256 devices in a mesh: own: 8 (over y_lo, x), br: 32 (over z, y_hi, core).
Axes of the slice: x: 4, y: 4 (y_hi: 2, y_lo: 2; y = y_hi * 2 + y_lo), z: 8, core: 2. Of those that a mesh axis runs over, the one named last changes fastest.
Arguments:
- queries: bfloat16 [128, 256, 5120], P('br', None, 'own'), may hold values from -6 to 6
- branch_keys: bfloat16 [128, 256, 1024], P('br', None, 'own'), may hold values from -6 to 6
- branch_values: bfloat16 [128, 256, 1024], P('br', None, 'own'), may hold values from -6 to 6
- attn_out: bfloat16 [128, 256, 5120], P('br', None, 'own'), may hold values from -6 to 6
- out_grad: bfloat16 [128, 256, 5120], P('br', None, 'own'), may hold values from -6 to 6
- logsumexp: float32 [128, 40, 256], P('br', 'own'), may hold values from 7 to 8.5
- prefix_keys: bfloat16 [512, 8, 1024], P('br', 'own'), may hold values from -6 to 6
- prefix_values: bfloat16 [512, 8, 1024], P('br', 'own'), may hold values from -6 to 6
- prefix_of: int32 [128], P('br'), may hold values from 0 to 7
- counts: int32 [32], P('br'), may hold values from 1 to 4, as said below
Outputs:
- query_grad: bfloat16 [128, 256, 5120], P('br', None, 'own')
- key_grad: bfloat16 [128, 256, 1024], P('br', None, 'own')
- value_grad: bfloat16 [128, 256, 1024], P('br', None, 'own')
- prefix_key_grad: bfloat16 [512, 8, 1024], P('br', 'own')
- prefix_value_grad: bfloat16 [512, 8, 1024], P('br', 'own')
The draws below stay inside these ranges and needn't reach their ends.
Inputs may be any that keep to these rules, and one draw needn't show every extreme that they name: The first counts[b] of the 4 slots of br index b hold branches, the other slots are empty; some br index is full in every draw.
All inputs are finite; a program needn't handle non-finite values.
Results may differ from the reference program's by a relative error of at most 0.0049.
Values may be sent and summed in bfloat16 or wider, within the bound.
No kernel may reach another device: no remote copies, remote signals or barrier semaphores. Data moves between devices by JAX's collectives and lax.ppermute only.
A program may use at most 64 MiB of HBM per device.

```python
import jax
import jax.numpy as jnp
from jax import lax

QH = 40
KVH = 8
HD = 128
CAP = 4
L = 256
P_SIZE = 512
NPRE = 8
SLOTS = 128
N_BR = 32


def draw_counts(key, part):
    key = jax.random.fold_in(key, 7)
    first, second = jax.random.split(key)
    picks = jax.random.randint(first, (N_BR,), 0, 4)
    values = jnp.where(picks == 0, CAP, 1).astype(jnp.int32)
    full_at = jax.random.randint(second, (), 0, N_BR)
    return values.at[full_at].set(CAP)


def with_ends(drawn, rng, least, high):
    longest = drawn.shape.index(max(drawn.shape))
    spots = []
    for shift in (0, 1):
        where = [jax.random.randint(jax.random.fold_in(rng, axis), (), 0, length) for axis, length in enumerate(drawn.shape)]
        where[longest] = (where[longest] + shift) % drawn.shape[longest]
        spots.append(tuple(where))
    return drawn.at[spots[0]].set(least).at[spots[1]].set(high)


def shard_levels(own_key, dims, cuts, low, largest):
    loudness, own = 1.0, jax.random.fold_in(own_key, 6)
    for dim, parts in cuts:
        heights = jnp.exp(jax.random.uniform(jax.random.fold_in(own, dim), (parts,), jnp.float32, low / len(cuts), largest / len(cuts)))
        loudness = loudness * jnp.repeat(heights, dims[dim] // parts).reshape([-1 if axis == dim else 1 for axis in range(len(dims))])
    return loudness


def normal_values(own_key, extent, width, bound, cuts=(), kind=jnp.bfloat16):
    array = width * jax.random.normal(own_key, extent, jnp.float32)
    if cuts:
        array = array * shard_levels(own_key, extent, cuts, -0.22, 0.18)
    return jnp.clip(array, -bound, bound).astype(kind)


def setup_inputs(seed: int = 0) -> dict:
    key_of = jax.random.split(jax.random.key(seed), 11)
    queries = normal_values(key_of[0], (SLOTS, L, QH * HD), 1.2, 6.0, ((0, 32), (2, 8)))
    branch_keys = normal_values(key_of[1], (SLOTS, L, KVH * HD), 1.2, 6.0, ((0, 32), (2, 8)))
    branch_values = normal_values(key_of[2], (SLOTS, L, KVH * HD), 1.0, 6.0, ((0, 32), (2, 8)))
    attn_out = normal_values(key_of[3], (SLOTS, L, QH * HD), 1.0, 6.0, ((0, 32), (2, 8)))
    out_grad = normal_values(key_of[4], (SLOTS, L, QH * HD), 2.0, 6.0, ((0, 32), (2, 8)))
    logsumexp = jnp.clip(7.0 + 1.5 * jax.random.uniform(key_of[5], (SLOTS, QH, L), jnp.float32) ** shard_levels(key_of[5], (SLOTS, QH, L), ((0, 32), (1, 8)), -0.2, 0.2), 7.0, 8.5)
    prefix_keys = normal_values(key_of[6], (P_SIZE, NPRE, KVH * HD), 1.2, 6.0, ((0, 32), (1, 8)))
    prefix_values = normal_values(key_of[7], (P_SIZE, NPRE, KVH * HD), 1.0, 6.0, ((0, 32), (1, 8)))
    prefix_of = with_ends(jax.random.randint(key_of[8], (SLOTS,), 0, NPRE), jax.random.fold_in(key_of[8], 1), 0, NPRE - 1).astype(jnp.int32)
    counts = draw_counts(jax.random.fold_in(key_of[10], 71), 0)
    return dict(queries=queries, branch_keys=branch_keys, branch_values=branch_values, attn_out=attn_out, out_grad=out_grad, logsumexp=logsumexp, prefix_keys=prefix_keys, prefix_values=prefix_values, prefix_of=prefix_of, counts=counts)


def reference(queries, branch_keys, branch_values, attn_out, out_grad, logsumexp, prefix_keys, prefix_values, prefix_of, counts):
    groups = QH // KVH
    scale = HD ** -0.5
    slot_ids = jnp.arange(SLOTS, dtype=jnp.int32)
    alive = ((slot_ids % CAP) < counts[slot_ids // CAP]).astype(jnp.float32)
    rows = jnp.arange(P_SIZE + L, dtype=jnp.int32)[None, :]
    tokens = jnp.arange(L, dtype=jnp.int32)[:, None]
    visible = (rows < P_SIZE) | (rows - P_SIZE <= tokens)

    def step(carry, item):
        pk_acc, pv_acc = carry
        query, bkey, bval, out, dout, lse, pidx, live = item
        pkey = lax.dynamic_index_in_dim(prefix_keys, pidx, 1, keepdims=False)
        pval = lax.dynamic_index_in_dim(prefix_values, pidx, 1, keepdims=False)
        all_keys = jnp.concatenate([pkey, bkey], 0).astype(jnp.float32).reshape(P_SIZE + L, KVH, HD)
        all_vals = jnp.concatenate([pval, bval], 0).astype(jnp.float32).reshape(P_SIZE + L, KVH, HD)
        q4 = query.astype(jnp.float32).reshape(L, KVH, groups, HD)
        d4 = dout.astype(jnp.float32).reshape(L, KVH, groups, HD)
        o4 = out.astype(jnp.float32).reshape(L, KVH, groups, HD)
        delta = jnp.einsum('lkgd,lkgd->kgl', d4, o4)
        score = jnp.einsum('lkgd,rkd->kglr', q4, all_keys) * scale
        lse4 = lse.reshape(KVH, groups, L)
        prob = jnp.where(visible, jnp.exp(score - lse4[..., None]), 0.0) * live
        prob_b = prob.astype(jnp.bfloat16).astype(jnp.float32)
        dprob = jnp.einsum('lkgd,rkd->kglr', d4, all_vals)
        dscore = (prob * (dprob - delta[..., None])).astype(jnp.bfloat16).astype(jnp.float32)
        dq = scale * jnp.einsum('kglr,rkd->lkgd', dscore, all_keys)
        dk = scale * jnp.einsum('kglr,lkgd->rkd', dscore, q4).reshape(P_SIZE + L, KVH * HD)
        dv = jnp.einsum('kglr,lkgd->rkd', prob_b, d4).reshape(P_SIZE + L, KVH * HD)
        old_k = lax.dynamic_index_in_dim(pk_acc, pidx, 1, keepdims=False)
        old_v = lax.dynamic_index_in_dim(pv_acc, pidx, 1, keepdims=False)
        pk_acc = lax.dynamic_update_index_in_dim(pk_acc, old_k + dk[:P_SIZE], pidx, 1)
        pv_acc = lax.dynamic_update_index_in_dim(pv_acc, old_v + dv[:P_SIZE], pidx, 1)
        outs = (dq.reshape(L, QH * HD).astype(jnp.bfloat16), dk[P_SIZE:].astype(jnp.bfloat16), dv[P_SIZE:].astype(jnp.bfloat16))
        return (pk_acc, pv_acc), outs

    zeros = jnp.zeros((P_SIZE, NPRE, KVH * HD), jnp.float32)
    items = (queries, branch_keys, branch_values, attn_out, out_grad, logsumexp, prefix_of, alive)
    (pk_acc, pv_acc), (dq_all, dk_all, dv_all) = lax.scan(step, (zeros, zeros), items)
    return dq_all, dk_all, dv_all, pk_acc.astype(jnp.bfloat16), pv_acc.astype(jnp.bfloat16)
```

```python
import functools

import jax
import jax.numpy as jnp
from jax import lax
from jax.experimental import pallas as pl
from jax.experimental.pallas import tpu as pltpu
from jax.sharding import PartitionSpec as P

QH = 40
KVH = 8
HD = 128
GROUPS = QH // KVH
SCALE = HD ** (-0.5)
NZ, NY, NC = 8, 2, 2
OWN = 8
MIB = 1 << 20


def br_index(z, y, c):
    return (z % NZ) * NY * NC + y * NC + c


def ring_perm(hops):
    return [
        (br_index(z, y, c), br_index(z + (hops if c == 0 else -hops), y, c))
        for z in range(NZ)
        for y in range(NY)
        for c in range(NC)
    ]


CORE_SWAP = [(i, i ^ 1) for i in range(NZ * NY * NC)]
PLANES = [
    [br_index(z, y, c) * OWN + o for y in range(NY) for c in range(NC) for o in range(OWN)]
    for z in range(NZ)
]


def plane_exchange(blocks):
    return lax.all_to_all(
        blocks, ("br", "own"), split_axis=0, concat_axis=0, tiled=True, axis_index_groups=PLANES
    )


def dot_nt(a, b):
    return lax.dot_general(a, b, (((1,), (1,)), ((), ())), preferred_element_type=jnp.float32)


def dot_nn(a, b):
    return lax.dot_general(a, b, (((1,), (0,)), ((), ())), preferred_element_type=jnp.float32)


def dot_tn(a, b):
    return lax.dot_general(a, b, (((0,), (0,)), ((), ())), preferred_element_type=jnp.float32)


def self_kernel(
    count_ref, q_ref, k_ref, v_ref, o_ref, do_ref, lse_ref, dq_ref, dk_ref, dv_ref, stat_ref
):
    slot = pl.program_id(0)
    live = slot < count_ref[0]

    @pl.when(live)
    def _():
        k = k_ref[0]
        v = v_ref[0]
        length = k.shape[0]
        row = lax.broadcasted_iota(jnp.int32, (length, length), 0)
        token = lax.broadcasted_iota(jnp.int32, (length, length), 1)
        visible = row <= token
        dk = jnp.zeros((length, HD), jnp.float32)
        dv = jnp.zeros((length, HD), jnp.float32)
        for g in range(GROUPS):
            cols = slice(g * HD, (g + 1) * HD)
            q = q_ref[0, :, cols]
            do = do_ref[0, :, cols]
            product = do.astype(jnp.float32) * o_ref[0, :, cols].astype(jnp.float32)
            delta = jnp.sum(product.T, axis=0, keepdims=True)
            lse = lse_ref[0, g : g + 1, :]
            stat_ref[0, g : g + 1, :] = lse
            stat_ref[0, 8 + g : 9 + g, :] = delta
            prob = jnp.where(visible, jnp.exp(dot_nt(k, q) * SCALE - lse), 0.0)
            dscore = (prob * (dot_nt(v, do) - delta)).astype(jnp.bfloat16)
            dk += dot_nn(dscore, q)
            dv += dot_nn(prob.astype(jnp.bfloat16), do)
            dq_ref[0, :, cols] = SCALE * dot_tn(dscore, k)
        dk_ref[0] = (SCALE * dk).astype(jnp.bfloat16)
        dv_ref[0] = dv.astype(jnp.bfloat16)

    @pl.when(jnp.logical_not(live))
    def _():
        dq_ref[...] = jnp.zeros_like(dq_ref)
        dk_ref[...] = jnp.zeros_like(dk_ref)
        dv_ref[...] = jnp.zeros_like(dv_ref)
        stat_ref[...] = jnp.zeros_like(stat_ref)


def self_part(count, queries, keys, values, attn_out, out_grad, logsumexp):
    slots, length, width = queries.shape

    def spec(*shape):
        return pl.BlockSpec((1,) + shape, lambda i, c: (i, 0, 0))

    wide, narrow = spec(length, width), spec(length, HD)
    return pl.pallas_call(
        self_kernel,
        grid_spec=pltpu.PrefetchScalarGridSpec(
            num_scalar_prefetch=1,
            grid=(slots,),
            in_specs=[wide, narrow, narrow, wide, wide, spec(GROUPS, length)],
            out_specs=[wide, narrow, narrow, spec(16, length)],
        ),
        out_shape=[
            jax.ShapeDtypeStruct((slots, length, width), jnp.float32),
            jax.ShapeDtypeStruct((slots, length, HD), jnp.bfloat16),
            jax.ShapeDtypeStruct((slots, length, HD), jnp.bfloat16),
            jax.ShapeDtypeStruct((slots, 16, length), jnp.float32),
        ],
        compiler_params=pltpu.CompilerParams(vmem_limit_bytes=32 * MIB),
        cost_estimate=pl.CostEstimate(
            flops=slots * 10 * length * length * width,
            bytes_accessed=slots * length * width * 10,
            transcendentals=slots * length * length * GROUPS,
        ),
        name="self_part",
    )(count, queries, keys, values, attn_out, out_grad, logsumexp)


def prefix_kernel(n_pieces, slots, pre_ref, *refs):
    q_own, do_own, stat_own, q_oth, do_oth, stat_oth = refs[:6]
    pieces = refs[6 : 6 + n_pieces]
    dq_own, dq_oth = refs[6 + n_pieces : 8 + n_pieces]
    outs = refs[8 + n_pieces : 8 + 2 * n_pieces]
    acc = refs[8 + 2 * n_pieces]
    step = pl.program_id(0)
    prefix = pre_ref[step]

    @pl.when(step == 0)
    def _():
        acc[...] = jnp.zeros_like(acc)

    def work(q_ref, do_ref, stat_ref, dq_ref):
        @pl.when(prefix >= 0)
        def _():
            rows = [p[:, prefix] for p in pieces]
            kv = jnp.concatenate([r.reshape(r.shape[0] * r.shape[1], 2 * HD) for r in rows], 0)
            k, v = kv[:, :HD], kv[:, HD:]
            dk = jnp.zeros(k.shape, jnp.float32)
            dv = jnp.zeros(v.shape, jnp.float32)
            for g in range(GROUPS):
                cols = slice(g * HD, (g + 1) * HD)
                q = q_ref[0, :, cols]
                do = do_ref[0, :, cols]
                lse = stat_ref[0, g : g + 1, :]
                delta = stat_ref[0, 8 + g : 9 + g, :]
                prob = jnp.exp(dot_nt(k, q) * SCALE - lse)
                dscore = (prob * (dot_nt(v, do) - delta)).astype(jnp.bfloat16)
                dk += dot_nn(dscore, q)
                dv += dot_nn(prob.astype(jnp.bfloat16), do)
                dq_ref[0, :, cols] = (SCALE * dot_tn(dscore, k)).astype(dq_ref.dtype)
            acc[prefix, :, :HD] += SCALE * dk
            acc[prefix, :, HD:] += dv

        @pl.when(prefix < 0)
        def _():
            dq_ref[...] = jnp.zeros_like(dq_ref)

    @pl.when(step < slots)
    def _():
        work(q_own, do_own, stat_own, dq_own)

    @pl.when(step >= slots)
    def _():
        work(q_oth, do_oth, stat_oth, dq_oth)

    @pl.when(step == 2 * slots - 1)
    def _():
        start = 0
        for out in outs:
            for block in range(out.shape[0]):
                out[block] = acc[:, start : start + out.shape[2], :].astype(out.dtype)
                start += out.shape[2]


def prefix_part(prefixes, own, oth, pieces):
    slots, length, width = own[0].shape
    n_rows = sum(p.shape[0] * p.shape[2] for p in pieces)
    n_pre = pieces[0].shape[1]

    def first(*shape):
        return pl.BlockSpec((1,) + shape, lambda i, c: (jnp.minimum(i, slots - 1), 0, 0))

    def second(*shape):
        return pl.BlockSpec((1,) + shape, lambda i, c: (jnp.maximum(i - slots, 0), 0, 0))

    def whole(p):
        return pl.BlockSpec(p.shape, lambda i, c: (0, 0, 0, 0))

    in_specs = []
    for place in (first, second):
        in_specs += [place(length, width), place(length, width), place(16, length)]
    return pl.pallas_call(
        functools.partial(prefix_kernel, len(pieces), slots),
        grid_spec=pltpu.PrefetchScalarGridSpec(
            num_scalar_prefetch=1,
            grid=(2 * slots,),
            in_specs=in_specs + [whole(p) for p in pieces],
            out_specs=[first(length, width), second(length, width)] + [whole(p) for p in pieces],
            scratch_shapes=[pltpu.VMEM((n_pre, n_rows, 2 * HD), jnp.float32)],
        ),
        out_shape=[
            jax.ShapeDtypeStruct((slots, length, width), jnp.float32),
            jax.ShapeDtypeStruct((slots, length, width), jnp.bfloat16),
        ]
        + [jax.ShapeDtypeStruct(p.shape, jnp.bfloat16) for p in pieces],
        compiler_params=pltpu.CompilerParams(vmem_limit_bytes=48 * MIB),
        cost_estimate=pl.CostEstimate(
            flops=2 * slots * 10 * length * n_rows * width,
            bytes_accessed=slots * length * width * 16,
            transcendentals=2 * slots * length * n_rows * GROUPS,
        ),
        name="prefix_part",
    )(prefixes, *own, *oth, *pieces)


def per_device(
    queries,
    branch_keys,
    branch_values,
    attn_out,
    out_grad,
    logsumexp,
    prefix_keys,
    prefix_values,
    prefix_of,
    counts,
):
    slots = queries.shape[0]
    rows, n_pre = prefix_keys.shape[0], OWN
    core = lax.rem(lax.axis_index("br"), NC)
    swap = functools.partial(lax.ppermute, axis_name="br", perm=CORE_SWAP)

    mine = jnp.where(jnp.arange(slots) < counts[0], prefix_of, -1)
    prefixes = jnp.concatenate([mine, swap(mine)])
    q_oth, do_oth = swap(queries), swap(out_grad)

    heads = jnp.concatenate(
        [prefix_keys.reshape(rows, KVH, HD), prefix_values.reshape(rows, KVH, HD)], 2
    ).transpose(1, 0, 2)
    sent = jnp.broadcast_to(heads[None], (NY * NC, KVH, rows, 2 * HD))
    plane = plane_exchange(sent.reshape(NY * NC * KVH, rows, 2 * HD))
    plane = plane.reshape(NY * NC, n_pre, rows, 2 * HD)

    def half(a):
        return lax.dynamic_slice_in_dim(a, core * (NY * NC // 2), NY * NC // 2, 0)

    own_half = half(plane)
    one = lax.ppermute(plane, "br", ring_perm(1))
    two = lax.ppermute(one, "br", ring_perm(1))
    three = lax.ppermute(two, "br", ring_perm(1))
    four = lax.ppermute(half(three), "br", ring_perm(1))

    dq_self, key_grad, value_grad, stat = self_part(
        counts, queries, branch_keys, branch_values, attn_out, out_grad, logsumexp
    )
    stat_oth = swap(stat)
    dq_own, dq_oth, g_own, g1, g2, g3, g4 = prefix_part(
        prefixes,
        (queries, out_grad, stat),
        (q_oth, do_oth, stat_oth),
        (own_half, one, two, three, four),
    )
    h4 = lax.ppermute(g4, "br", ring_perm(-4))
    h3 = lax.ppermute(g3, "br", ring_perm(-3))
    h2 = lax.ppermute(g2, "br", ring_perm(-2))
    h1 = lax.ppermute(g1, "br", ring_perm(-1))
    dq_back = swap(dq_oth)

    f32 = jnp.float32
    halves = g_own.astype(f32) + h4.astype(f32)
    in_half = (jnp.arange(NY * NC) // (NY * NC // 2) == core)[:, None, None, None]
    spread = jnp.where(in_half, jnp.concatenate([halves, halves], 0), 0.0)
    total = (h1.astype(f32) + h2.astype(f32)) + (h3.astype(f32) + spread)
    total = total.astype(jnp.bfloat16).reshape(NY * NC * n_pre, rows, 2 * HD)
    home = plane_exchange(total).reshape(NY * NC, KVH, rows, 2 * HD)
    home = jnp.sum(home.astype(f32), axis=0).astype(jnp.bfloat16).transpose(1, 0, 2)
    prefix_key_grad = home[:, :, :HD].reshape(rows, 1, KVH * HD)
    prefix_value_grad = home[:, :, HD:].reshape(rows, 1, KVH * HD)
    query_grad = (dq_self + dq_own + dq_back.astype(f32)).astype(jnp.bfloat16)
    return (query_grad, key_grad, value_grad, prefix_key_grad, prefix_value_grad)


def solution(mesh):
    placed = (
        P("br", None, "own"),
        P("br", None, "own"),
        P("br", None, "own"),
        P("br", None, "own"),
        P("br", None, "own"),
        P("br", "own", None),
        P("br", "own", None),
        P("br", "own", None),
        P("br"),
        P("br"),
    )
    return jax.shard_map(
        per_device,
        mesh=mesh,
        in_specs=placed,
        out_specs=(
            P("br", None, "own"),
            P("br", None, "own"),
            P("br", None, "own"),
            P("br", "own", None),
            P("br", "own", None),
        ),
        check_vma=False,
    )
```

```python
import functools

import jax
import jax.numpy as jnp
from jax import lax
from jax.experimental import pallas as pl
from jax.experimental.pallas import tpu as pltpu
from jax.sharding import PartitionSpec as P

QH = 40
KVH = 8
HD = 128
GROUPS = QH // KVH
SCALE = HD ** (-0.5)
NZ, NY, NC = 8, 2, 2
OWN = 8
KERNEL_VMEM = 24 << 20
NZ, NY, NC = 8, 2, 2
OWN = 8
KERNEL_VMEM = 24 << 20
NEAR_WEIGHT = 0.01


def br_index(z, y, c):
    return (z % NZ) * NY * NC + y * NC + c


def ring_perm(hops):
    return [
        (br_index(z, y, c), br_index(z + (hops if c == 0 else -hops), y, c))
        for z in range(NZ)
        for y in range(NY)
        for c in range(NC)
    ]


CORE_SWAP = [(i, i ^ 1) for i in range(NZ * NY * NC)]
PLANES = [
    [br_index(z, y, c) * OWN + o for y in range(NY) for c in range(NC) for o in range(OWN)]
    for z in range(NZ)
]


def plane_exchange(blocks):
    return lax.all_to_all(
        blocks, ("br", "own"), split_axis=0, concat_axis=0, tiled=True, axis_index_groups=PLANES
    )


def dot_nt(a, b):
    return lax.dot_general(a, b, (((1,), (1,)), ((), ())), preferred_element_type=jnp.float32)


def dot_nn(a, b):
    return lax.dot_general(a, b, (((1,), (0,)), ((), ())), preferred_element_type=jnp.float32)


def dot_tn(a, b):
    return lax.dot_general(a, b, (((0,), (0,)), ((), ())), preferred_element_type=jnp.float32)


def heads_of(ref, slot):
    return [ref[slot, :, g * HD : (g + 1) * HD] for g in range(GROUPS)]


def attention_grads(k, v, qs, dos, lses, deltas, visible=None):
    probs = [jnp.exp(dot_nt(k, q) * SCALE - lse) for q, lse in zip(qs, lses)]
    if visible is not None:
        probs = [jnp.where(visible, prob, 0.0) for prob in probs]
    dprobs = [dot_nt(v, do) for do in dos]
    dscores = [
        (prob * (dprob - delta)).astype(jnp.bfloat16)
        for prob, dprob, delta in zip(probs, dprobs, deltas)
    ]
    probs = [prob.astype(jnp.bfloat16) for prob in probs]
    dk = SCALE * dot_nn(jnp.concatenate(dscores, 1), jnp.concatenate(qs, 0))
    dv = dot_nn(jnp.concatenate(probs, 1), jnp.concatenate(dos, 0))
    dqs = [SCALE * dot_tn(dscore, k) for dscore in dscores]
    return dqs, dk, dv


def vmem():
    return pl.BlockSpec(memory_space=pltpu.VMEM)


def smem():
    return pl.BlockSpec(memory_space=pltpu.SMEM)


def send_kernel(key_ref, value_ref, out_ref):
    for h in range(KVH):
        cols = slice(h * HD, (h + 1) * HD)
        key, value = key_ref[:, cols], value_ref[:, cols]
        for block in range(NY * NC):
            out_ref[block * KVH + h, :, :HD] = key
            out_ref[block * KVH + h, :, HD:] = value


def send_part(prefix_keys, prefix_values):
    rows = prefix_keys.shape[0]
    flat = (rows, KVH * HD)
    return pl.pallas_call(
        send_kernel,
        in_specs=[vmem()] * 2,
        out_specs=vmem(),
        out_shape=jax.ShapeDtypeStruct((NY * NC * KVH, rows, 2 * HD), jnp.bfloat16),
        name="send_part",
    )(prefix_keys.reshape(flat), prefix_values.reshape(flat))


def home_kernel(in_ref, key_ref, value_ref):
    for h in range(KVH):
        cols = slice(h * HD, (h + 1) * HD)
        parts = [in_ref[block * KVH + h].astype(jnp.float32) for block in range(NY * NC)]
        total = ((parts[0] + parts[1]) + (parts[2] + parts[3])).astype(jnp.bfloat16)
        key_ref[:, cols] = total[:, :HD]
        value_ref[:, cols] = total[:, HD:]


def home_part(received):
    rows = received.shape[1]
    shape = jax.ShapeDtypeStruct((rows, KVH * HD), jnp.bfloat16)
    grads = pl.pallas_call(
        home_kernel,
        in_specs=[vmem()],
        out_specs=[vmem()] * 2,
        out_shape=[shape, shape],
        name="home_part",
    )(received)
    return [grad.reshape(rows, 1, KVH * HD) for grad in grads]


def self_kernel(
    count_ref, q_ref, k_ref, v_ref, o_ref, do_ref, lse_ref, dq_ref, dk_ref, dv_ref, stat_ref
):
    live = pl.program_id(0) < count_ref[0]

    @pl.when(live)
    def _():
        k, v = k_ref[0], v_ref[0]
        length = k.shape[0]
        row = lax.broadcasted_iota(jnp.int32, (length, length), 0)
        token = lax.broadcasted_iota(jnp.int32, (length, length), 1)
        qs, dos, outs = heads_of(q_ref, 0), heads_of(do_ref, 0), heads_of(o_ref, 0)
        lses = [lse_ref[0, g : g + 1, :] for g in range(GROUPS)]
        deltas = [
            jnp.sum((do.astype(jnp.float32) * o.astype(jnp.float32)).T, axis=0, keepdims=True)
            for do, o in zip(dos, outs)
        ]
        for g in range(GROUPS):
            stat_ref[0, g : g + 1, :] = lses[g]
            stat_ref[0, 8 + g : 9 + g, :] = deltas[g]
        dqs, dk, dv = attention_grads(k, v, qs, dos, lses, deltas, row <= token)
        for g in range(GROUPS):
            dq_ref[0, :, g * HD : (g + 1) * HD] = dqs[g].astype(dq_ref.dtype)
        dk_ref[0] = dk.astype(jnp.bfloat16)
        dv_ref[0] = dv.astype(jnp.bfloat16)

    @pl.when(jnp.logical_not(live))
    def _():
        for ref in (dq_ref, dk_ref, dv_ref, stat_ref):
            ref[...] = jnp.zeros_like(ref)


def self_part(count, queries, keys, values, attn_out, out_grad, logsumexp):
    slots, length, width = queries.shape

    def spec(*shape):
        return pl.BlockSpec((1,) + shape, lambda i: (i, 0, 0))

    wide, narrow = spec(length, width), spec(length, HD)
    return pl.pallas_call(
        self_kernel,
        grid=(slots,),
        in_specs=[smem(), wide, narrow, narrow, wide, wide, spec(GROUPS, length)],
        out_specs=[wide, narrow, narrow, spec(16, length)],
        out_shape=[
            jax.ShapeDtypeStruct((slots, length, width), jnp.bfloat16),
            jax.ShapeDtypeStruct((slots, length, HD), jnp.bfloat16),
            jax.ShapeDtypeStruct((slots, length, HD), jnp.bfloat16),
            jax.ShapeDtypeStruct((slots, 16, length), jnp.float32),
        ],
        compiler_params=pltpu.CompilerParams(vmem_limit_bytes=KERNEL_VMEM),
        cost_estimate=pl.CostEstimate(
            flops=slots * 10 * length * length * width,
            bytes_accessed=slots * length * width * 10,
            transcendentals=slots * length * length * GROUPS,
        ),
        name="self_part",
    )(count, queries, keys, values, attn_out, out_grad, logsumexp)


def prefix_kernel(n_pieces, slots, with_oth, pre_ref, *refs):
    refs = list(refs)
    take = lambda n: [refs.pop(0) for _ in range(n)]
    q_own, do_own, stat_own, q_oth, do_oth, stat_oth, more_own = take(7)
    more_oth = take(1)[0] if with_oth else None
    pieces = take(n_pieces)
    dq_own, dq_oth = take(2)
    outs = take(n_pieces)
    (acc,) = refs
    step = pl.program_id(0)
    prefix = pre_ref[step]

    @pl.when(step == 0)
    def _():
        acc[...] = jnp.zeros_like(acc)

    def work(q_ref, do_ref, stat_ref, more_ref, dq_ref):
        @pl.when(prefix >= 0)
        def _():
            rows = [p[:, prefix] for p in pieces]
            kv = jnp.concatenate([r.reshape(r.shape[0] * r.shape[1], 2 * HD) for r in rows], 0)
            k, v = kv[:, :HD], kv[:, HD:]
            dqs, dk, dv = attention_grads(
                k,
                v,
                heads_of(q_ref, 0),
                heads_of(do_ref, 0),
                [stat_ref[0, g : g + 1, :] for g in range(GROUPS)],
                [stat_ref[0, 8 + g : 9 + g, :] for g in range(GROUPS)],
            )
            for g in range(GROUPS):
                cols = slice(g * HD, (g + 1) * HD)
                dq = dqs[g]
                if more_ref is not None:
                    dq += more_ref[0, :, cols].astype(jnp.float32)
                dq_ref[0, :, cols] = dq.astype(dq_ref.dtype)
            acc[prefix, :, :HD] += dk
            acc[prefix, :, HD:] += dv

        @pl.when(prefix < 0)
        def _():
            dq_ref[...] = jnp.zeros_like(dq_ref)

    @pl.when(step < slots)
    def _():
        work(q_own, do_own, stat_own, more_own, dq_own)

    @pl.when(step >= slots)
    def _():
        work(q_oth, do_oth, stat_oth, more_oth, dq_oth)

    @pl.when(step == 2 * slots - 1)
    def _():
        start = 0
        for out in outs:
            for block in range(out.shape[0]):
                out[block] = acc[:, start : start + out.shape[2], :].astype(out.dtype)
                start += out.shape[2]


def prefix_part(prefixes, own, oth, pieces, name):
    slots, length, width = own[0].shape
    n_rows = sum(p.shape[0] * p.shape[2] for p in pieces)
    n_pre = pieces[0].shape[1]

    def first(*shape):
        return pl.BlockSpec((1,) + shape, lambda i, c: (jnp.minimum(i, slots - 1), 0, 0))

    def second(*shape):
        return pl.BlockSpec((1,) + shape, lambda i, c: (jnp.maximum(i - slots, 0), 0, 0))

    def whole(p):
        return pl.BlockSpec(p.shape, lambda i, c: (0, 0, 0, 0))

    in_specs = [first(*a.shape[1:]) for a in own[:3]] + [second(*a.shape[1:]) for a in oth[:3]]
    in_specs += [first(length, width)] + [second(length, width) for _ in oth[3:]]
    return pl.pallas_call(
        functools.partial(prefix_kernel, len(pieces), slots, len(oth) > 3),
        grid_spec=pltpu.PrefetchScalarGridSpec(
            num_scalar_prefetch=1,
            grid=(2 * slots,),
            in_specs=in_specs + [whole(p) for p in pieces],
            out_specs=[first(length, width), second(length, width)] + [whole(p) for p in pieces],
            scratch_shapes=[pltpu.VMEM((n_pre, n_rows, 2 * HD), jnp.float32)],
        ),
        out_shape=[
            jax.ShapeDtypeStruct((slots, length, width), jnp.bfloat16),
            jax.ShapeDtypeStruct((slots, length, width), jnp.bfloat16),
        ]
        + [jax.ShapeDtypeStruct(p.shape, jnp.bfloat16) for p in pieces],
        compiler_params=pltpu.CompilerParams(vmem_limit_bytes=KERNEL_VMEM),
        cost_estimate=pl.CostEstimate(
            flops=2 * slots * 10 * length * n_rows * width,
            bytes_accessed=slots * length * width * 16,
            transcendentals=2 * slots * length * n_rows * GROUPS,
        ),
        name=name,
    )(prefixes, *own[:3], *oth[:3], own[3], *oth[3:], *pieces)


def per_device(
    queries,
    branch_keys,
    branch_values,
    attn_out,
    out_grad,
    logsumexp,
    prefix_keys,
    prefix_values,
    prefix_of,
    counts,
):
    slots = queries.shape[0]
    rows, n_pre = prefix_keys.shape[0], OWN
    core = lax.rem(lax.axis_index("br"), NC)
    swap = functools.partial(lax.ppermute, axis_name="br", perm=CORE_SWAP)

    f32, bf16 = jnp.float32, jnp.bfloat16
    plane = plane_exchange(send_part(prefix_keys, prefix_values))
    plane = plane.reshape(NY * NC, n_pre, rows, 2 * HD)

    mine = jnp.where(jnp.arange(slots) < counts[0], prefix_of, -1)
    prefixes = jnp.concatenate([mine, swap(mine)])
    q_oth, do_oth = swap(queries), swap(out_grad)
    plane, prefixes, q_oth, do_oth, count = lax.optimization_barrier(
        (plane, prefixes, q_oth, do_oth, counts)
    )
    own_half = lax.dynamic_slice_in_dim(plane, core * (NY * NC // 2), NY * NC // 2, 0)
    one = lax.ppermute(plane, "br", ring_perm(1))
    two = lax.ppermute(plane, "br", ring_perm(2))
    three = lax.ppermute(one, "br", ring_perm(2))
    two_half = lax.dynamic_slice_in_dim(two, core * (NY * NC // 2), NY * NC // 2, 0)
    four = lax.ppermute(two_half, "br", ring_perm(2))
    dq_self, key_grad, value_grad, stat = self_part(
        count, queries, branch_keys, branch_values, attn_out, out_grad, logsumexp
    )
    stat_oth = swap(stat)
    dq_own, dq_oth, g_own, g1, g2, g3, g4 = prefix_part(
        prefixes,
        (queries, out_grad, stat, dq_self),
        (q_oth, do_oth, stat_oth),
        (own_half, one, two, three, four),
        "prefix_part",
    )
    h4 = lax.ppermute(g4, "br", ring_perm(-4))
    h3 = lax.ppermute(g3, "br", ring_perm(-3))
    h2 = lax.ppermute(g2, "br", ring_perm(-2))
    h1 = lax.ppermute(g1, "br", ring_perm(-1))
    dq_back = swap(dq_oth)
    query_grad = (dq_own.astype(f32) + dq_back.astype(f32)).astype(bf16)

    in_half = (jnp.arange(NY * NC) // (NY * NC // 2) == core)[:, None, None, None]
    halves = g_own.astype(f32) + h4.astype(f32)
    spread = jnp.where(in_half, jnp.concatenate([halves, halves], 0), 0.0)
    near = h1.astype(f32) + h2.astype(f32)
    total = (near + (h3.astype(f32) + spread)).astype(bf16)
    total, query_grad = lax.optimization_barrier((total, query_grad))
    prefix_key_grad, prefix_value_grad = home_part(
        plane_exchange(total.reshape(NY * NC * n_pre, rows, 2 * HD))
    )
    return (query_grad, key_grad, value_grad, prefix_key_grad, prefix_value_grad)


def solution(mesh):
    placed = (
        P("br", None, "own"),
        P("br", None, "own"),
        P("br", None, "own"),
        P("br", None, "own"),
        P("br", None, "own"),
        P("br", "own", None),
        P("br", "own", None),
        P("br", "own", None),
        P("br"),
        P("br"),
    )
    return jax.shard_map(
        per_device,
        mesh=mesh,
        in_specs=placed,
        out_specs=(
            P("br", None, "own"),
            P("br", None, "own"),
            P("br", None, "own"),
            P("br", "own", None),
            P("br", "own", None),
        ),
        check_vma=False,
    )
```

```python
import functools

import jax
import jax.numpy as jnp
from jax import lax
from jax.experimental import pallas as pl
from jax.experimental.pallas import tpu as pltpu
from jax.sharding import PartitionSpec as P

QH = 40
KVH = 8
HD = 128
GROUPS = QH // KVH
SCALE = HD ** (-0.5)
NZ, NY, NC = 8, 2, 2
OWN = 8
KERNEL_VMEM = 24 << 20
NZ, NY, NC = 8, 2, 2
OWN = 8
KERNEL_VMEM = 24 << 20
NEAR_WEIGHT = 0.01


def br_index(z, y, c):
    return (z % NZ) * NY * NC + y * NC + c


def ring_perm(hops):
    return [
        (br_index(z, y, c), br_index(z + (hops if c == 0 else -hops), y, c))
        for z in range(NZ)
        for y in range(NY)
        for c in range(NC)
    ]


CORE_SWAP = [(i, i ^ 1) for i in range(NZ * NY * NC)]
PLANES = [
    [br_index(z, y, c) * OWN + o for y in range(NY) for c in range(NC) for o in range(OWN)]
    for z in range(NZ)
]


def plane_exchange(blocks):
    return lax.all_to_all(
        blocks, ("br", "own"), split_axis=0, concat_axis=0, tiled=True, axis_index_groups=PLANES
    )


def dot_nt(a, b):
    return lax.dot_general(a, b, (((1,), (1,)), ((), ())), preferred_element_type=jnp.float32)


def dot_nn(a, b):
    return lax.dot_general(a, b, (((1,), (0,)), ((), ())), preferred_element_type=jnp.float32)


def dot_tn(a, b):
    return lax.dot_general(a, b, (((0,), (0,)), ((), ())), preferred_element_type=jnp.float32)


def heads_of(ref, slot):
    return [ref[slot, :, g * HD : (g + 1) * HD] for g in range(GROUPS)]


def attention_grads(k, v, qs, dos, lses, deltas, visible=None):
    probs = [jnp.exp(dot_nt(k, q) * SCALE - lse) for q, lse in zip(qs, lses)]
    if visible is not None:
        probs = [jnp.where(visible, prob, 0.0) for prob in probs]
    dprobs = [dot_nt(v, do) for do in dos]
    dscores = [
        (prob * (dprob - delta)).astype(jnp.bfloat16)
        for prob, dprob, delta in zip(probs, dprobs, deltas)
    ]
    probs = [prob.astype(jnp.bfloat16) for prob in probs]
    dk = SCALE * dot_nn(jnp.concatenate(dscores, 1), jnp.concatenate(qs, 0))
    dv = dot_nn(jnp.concatenate(probs, 1), jnp.concatenate(dos, 0))
    dqs = [SCALE * dot_tn(dscore, k) for dscore in dscores]
    return dqs, dk, dv


def vmem():
    return pl.BlockSpec(memory_space=pltpu.VMEM)


def smem():
    return pl.BlockSpec(memory_space=pltpu.SMEM)


def send_kernel(key_ref, value_ref, out_ref):
    for h in range(KVH):
        cols = slice(h * HD, (h + 1) * HD)
        key, value = key_ref[:, cols], value_ref[:, cols]
        for block in range(NY * NC):
            out_ref[block * KVH + h, :, :HD] = key
            out_ref[block * KVH + h, :, HD:] = value


def send_part(prefix_keys, prefix_values):
    rows = prefix_keys.shape[0]
    flat = (rows, KVH * HD)
    return pl.pallas_call(
        send_kernel,
        in_specs=[vmem()] * 2,
        out_specs=vmem(),
        out_shape=jax.ShapeDtypeStruct((NY * NC * KVH, rows, 2 * HD), jnp.bfloat16),
        name="send_part",
    )(prefix_keys.reshape(flat), prefix_values.reshape(flat))


def home_kernel(in_ref, key_ref, value_ref):
    for h in range(KVH):
        cols = slice(h * HD, (h + 1) * HD)
        parts = [in_ref[block * KVH + h].astype(jnp.float32) for block in range(NY * NC)]
        total = ((parts[0] + parts[1]) + (parts[2] + parts[3])).astype(jnp.bfloat16)
        key_ref[:, cols] = total[:, :HD]
        value_ref[:, cols] = total[:, HD:]


def home_part(received):
    rows = received.shape[1]
    shape = jax.ShapeDtypeStruct((rows, KVH * HD), jnp.bfloat16)
    grads = pl.pallas_call(
        home_kernel,
        in_specs=[vmem()],
        out_specs=[vmem()] * 2,
        out_shape=[shape, shape],
        name="home_part",
    )(received)
    return [grad.reshape(rows, 1, KVH * HD) for grad in grads]


def slot_spec(*shape):
    return pl.BlockSpec((1,) + shape, lambda i: (i, 0, 0))


def stat_kernel(o_ref, do_ref, lse_ref, stat_ref):
    stat_ref[0, :GROUPS, :] = lse_ref[0]
    for g, (do, o) in enumerate(zip(heads_of(do_ref, 0), heads_of(o_ref, 0))):
        product = do.astype(jnp.float32) * o.astype(jnp.float32)
        stat_ref[0, 8 + g : 9 + g, :] = jnp.sum(product.T, axis=0, keepdims=True)


def stat_part(attn_out, out_grad, logsumexp):
    slots, length, width = attn_out.shape
    return pl.pallas_call(
        stat_kernel,
        grid=(slots,),
        in_specs=[slot_spec(length, width), slot_spec(length, width), slot_spec(GROUPS, length)],
        out_specs=slot_spec(16, length),
        out_shape=jax.ShapeDtypeStruct((slots, 16, length), jnp.float32),
        compiler_params=pltpu.CompilerParams(vmem_limit_bytes=KERNEL_VMEM),
        cost_estimate=pl.CostEstimate(
            flops=slots * 2 * length * width,
            bytes_accessed=slots * length * width * 4,
            transcendentals=0,
        ),
        name="stat_part",
    )(attn_out, out_grad, logsumexp)


def self_kernel(count_ref, q_ref, k_ref, v_ref, do_ref, stat_ref, dq_ref, dk_ref, dv_ref):
    live = pl.program_id(0) < count_ref[0]

    @pl.when(live)
    def _():
        k, v = k_ref[0], v_ref[0]
        length = k.shape[0]
        row = lax.broadcasted_iota(jnp.int32, (length, length), 0)
        token = lax.broadcasted_iota(jnp.int32, (length, length), 1)
        dqs, dk, dv = attention_grads(
            k,
            v,
            heads_of(q_ref, 0),
            heads_of(do_ref, 0),
            [stat_ref[0, g : g + 1, :] for g in range(GROUPS)],
            [stat_ref[0, 8 + g : 9 + g, :] for g in range(GROUPS)],
            row <= token,
        )
        for g in range(GROUPS):
            dq_ref[0, :, g * HD : (g + 1) * HD] = dqs[g].astype(dq_ref.dtype)
        dk_ref[0] = dk.astype(jnp.bfloat16)
        dv_ref[0] = dv.astype(jnp.bfloat16)

    @pl.when(jnp.logical_not(live))
    def _():
        for ref in (dq_ref, dk_ref, dv_ref):
            ref[...] = jnp.zeros_like(ref)


def self_part(count, queries, keys, values, out_grad, stat):
    slots, length, width = queries.shape
    wide, narrow = slot_spec(length, width), slot_spec(length, HD)
    return pl.pallas_call(
        self_kernel,
        grid=(slots,),
        in_specs=[smem(), wide, narrow, narrow, wide, slot_spec(16, length)],
        out_specs=[wide, narrow, narrow],
        out_shape=[
            jax.ShapeDtypeStruct((slots, length, width), jnp.bfloat16),
            jax.ShapeDtypeStruct((slots, length, HD), jnp.bfloat16),
            jax.ShapeDtypeStruct((slots, length, HD), jnp.bfloat16),
        ],
        compiler_params=pltpu.CompilerParams(vmem_limit_bytes=KERNEL_VMEM),
        cost_estimate=pl.CostEstimate(
            flops=slots * 10 * length * length * width,
            bytes_accessed=slots * length * width * 10,
            transcendentals=slots * length * length * GROUPS,
        ),
        name="self_part",
    )(count, queries, keys, values, out_grad, stat)


def prefix_kernel(n_pieces, slots, with_oth, pre_ref, *refs):
    refs = list(refs)
    take = lambda n: [refs.pop(0) for _ in range(n)]
    q_own, do_own, stat_own, q_oth, do_oth, stat_oth, more_own = take(7)
    more_oth = take(1)[0] if with_oth else None
    pieces = take(n_pieces)
    dq_own, dq_oth = take(2)
    outs = take(n_pieces)
    (acc,) = refs
    step = pl.program_id(0)
    prefix = pre_ref[step]

    @pl.when(step == 0)
    def _():
        acc[...] = jnp.zeros_like(acc)

    def work(q_ref, do_ref, stat_ref, more_ref, dq_ref):
        @pl.when(prefix >= 0)
        def _():
            rows = [p[:, prefix] for p in pieces]
            kv = jnp.concatenate([r.reshape(r.shape[0] * r.shape[1], 2 * HD) for r in rows], 0)
            k, v = kv[:, :HD], kv[:, HD:]
            dqs, dk, dv = attention_grads(
                k,
                v,
                heads_of(q_ref, 0),
                heads_of(do_ref, 0),
                [stat_ref[0, g : g + 1, :] for g in range(GROUPS)],
                [stat_ref[0, 8 + g : 9 + g, :] for g in range(GROUPS)],
            )
            for g in range(GROUPS):
                cols = slice(g * HD, (g + 1) * HD)
                dq = dqs[g]
                if more_ref is not None:
                    dq += more_ref[0, :, cols].astype(jnp.float32)
                dq_ref[0, :, cols] = dq.astype(dq_ref.dtype)
            acc[prefix, :, :HD] += dk
            acc[prefix, :, HD:] += dv

        @pl.when(prefix < 0)
        def _():
            dq_ref[...] = jnp.zeros_like(dq_ref)

    @pl.when(step < slots)
    def _():
        work(q_own, do_own, stat_own, more_own, dq_own)

    @pl.when(step >= slots)
    def _():
        work(q_oth, do_oth, stat_oth, more_oth, dq_oth)

    @pl.when(step == 2 * slots - 1)
    def _():
        start = 0
        for out in outs:
            for block in range(out.shape[0]):
                out[block] = acc[:, start : start + out.shape[2], :].astype(out.dtype)
                start += out.shape[2]


def prefix_part(prefixes, own, oth, pieces, name):
    slots, length, width = own[0].shape
    n_rows = sum(p.shape[0] * p.shape[2] for p in pieces)
    n_pre = pieces[0].shape[1]

    def first(*shape):
        return pl.BlockSpec((1,) + shape, lambda i, c: (jnp.minimum(i, slots - 1), 0, 0))

    def second(*shape):
        return pl.BlockSpec((1,) + shape, lambda i, c: (jnp.maximum(i - slots, 0), 0, 0))

    def whole(p):
        return pl.BlockSpec(p.shape, lambda i, c: (0, 0, 0, 0))

    in_specs = [first(*a.shape[1:]) for a in own[:3]] + [second(*a.shape[1:]) for a in oth[:3]]
    in_specs += [first(length, width)] + [second(length, width) for _ in oth[3:]]
    return pl.pallas_call(
        functools.partial(prefix_kernel, len(pieces), slots, len(oth) > 3),
        grid_spec=pltpu.PrefetchScalarGridSpec(
            num_scalar_prefetch=1,
            grid=(2 * slots,),
            in_specs=in_specs + [whole(p) for p in pieces],
            out_specs=[first(length, width), second(length, width)] + [whole(p) for p in pieces],
            scratch_shapes=[pltpu.VMEM((n_pre, n_rows, 2 * HD), jnp.float32)],
        ),
        out_shape=[
            jax.ShapeDtypeStruct((slots, length, width), jnp.bfloat16),
            jax.ShapeDtypeStruct((slots, length, width), jnp.bfloat16),
        ]
        + [jax.ShapeDtypeStruct(p.shape, jnp.bfloat16) for p in pieces],
        compiler_params=pltpu.CompilerParams(vmem_limit_bytes=KERNEL_VMEM),
        cost_estimate=pl.CostEstimate(
            flops=2 * slots * 10 * length * n_rows * width,
            bytes_accessed=slots * length * width * 16,
            transcendentals=2 * slots * length * n_rows * GROUPS,
        ),
        name=name,
    )(prefixes, *own[:3], *oth[:3], own[3], *oth[3:], *pieces)


def per_device(
    queries,
    branch_keys,
    branch_values,
    attn_out,
    out_grad,
    logsumexp,
    prefix_keys,
    prefix_values,
    prefix_of,
    counts,
):
    slots = queries.shape[0]
    rows, n_pre = prefix_keys.shape[0], OWN
    core = lax.rem(lax.axis_index("br"), NC)
    swap = functools.partial(lax.ppermute, axis_name="br", perm=CORE_SWAP)

    f32, bf16 = jnp.float32, jnp.bfloat16
    plane = plane_exchange(send_part(prefix_keys, prefix_values))
    plane = plane.reshape(NY * NC, n_pre, rows, 2 * HD)

    mine = jnp.where(jnp.arange(slots) < counts[0], prefix_of, -1)
    prefixes = jnp.concatenate([mine, swap(mine)])
    q_oth, do_oth = swap(queries), swap(out_grad)
    stat = stat_part(attn_out, out_grad, logsumexp)
    stat_oth = swap(stat)
    plane, prefixes, q_oth, do_oth, count, stat, stat_oth = lax.optimization_barrier(
        (plane, prefixes, q_oth, do_oth, counts, stat, stat_oth)
    )
    own_half = lax.dynamic_slice_in_dim(plane, core * (NY * NC // 2), NY * NC // 2, 0)
    one = lax.ppermute(plane, "br", ring_perm(1))
    two = lax.ppermute(plane, "br", ring_perm(2))
    three = lax.ppermute(plane, "br", ring_perm(3))
    half_three = lax.dynamic_slice_in_dim(three, core * (NY * NC // 2), NY * NC // 2, 0)
    four = lax.ppermute(half_three, "br", ring_perm(1))
    dq_self, key_grad, value_grad = self_part(
        count, queries, branch_keys, branch_values, out_grad, stat
    )
    dq_own, dq_oth, g_own, g1, g2, g3, g4 = prefix_part(
        prefixes,
        (queries, out_grad, stat, dq_self),
        (q_oth, do_oth, stat_oth),
        (own_half, one, two, three, four),
        "prefix_part",
    )
    in_half = (jnp.arange(NY * NC) // (NY * NC // 2) == core)[:, None, None, None]
    far = lax.ppermute(g4, "br", ring_perm(-1)).astype(f32)
    far = jnp.where(in_half, jnp.concatenate([far, far], 0), 0.0)
    h3 = lax.ppermute((g3.astype(f32) + far).astype(bf16), "br", ring_perm(-3))
    h2 = lax.ppermute(g2, "br", ring_perm(-2))
    h1 = lax.ppermute(g1, "br", ring_perm(-1))
    dq_back = swap(dq_oth)
    query_grad = (dq_own.astype(f32) + dq_back.astype(f32)).astype(bf16)

    near, query_grad = lax.optimization_barrier((h1.astype(f32) + h2.astype(f32), query_grad))
    halves = g_own.astype(f32)
    spread = jnp.where(in_half, jnp.concatenate([halves, halves], 0), 0.0)
    total = (near + (h3.astype(f32) + spread)).astype(bf16)
    prefix_key_grad, prefix_value_grad = home_part(
        plane_exchange(total.reshape(NY * NC * n_pre, rows, 2 * HD))
    )
    return (query_grad, key_grad, value_grad, prefix_key_grad, prefix_value_grad)


def solution(mesh):
    placed = (
        P("br", None, "own"),
        P("br", None, "own"),
        P("br", None, "own"),
        P("br", None, "own"),
        P("br", None, "own"),
        P("br", "own", None),
        P("br", "own", None),
        P("br", "own", None),
        P("br"),
        P("br"),
    )
    return jax.shard_map(
        per_device,
        mesh=mesh,
        in_specs=placed,
        out_specs=(
            P("br", None, "own"),
            P("br", None, "own"),
            P("br", None, "own"),
            P("br", "own", None),
            P("br", "own", None),
        ),
        check_vma=False,
    )
```

```python
import functools

import jax
import jax.numpy as jnp
from jax import lax
from jax.experimental import pallas as pl
from jax.experimental.pallas import tpu as pltpu
from jax.sharding import PartitionSpec as P

QH = 40
KVH = 8
HD = 128
GROUPS = QH // KVH
SCALE = HD ** (-0.5)
LOG2E = 1.4426950408889634
NZ, NY, NC = 8, 2, 2
OWN = 8
KERNEL_VMEM = 24 << 20
NZ, NY, NC = 8, 2, 2
OWN = 8
KERNEL_VMEM = 24 << 20
NEAR_WEIGHT = 0.01


def br_index(z, y, c):
    return (z % NZ) * NY * NC + y * NC + c


def ring_perm(hops):
    return [
        (br_index(z, y, c), br_index(z + (hops if c == 0 else -hops), y, c))
        for z in range(NZ)
        for y in range(NY)
        for c in range(NC)
    ]


CORE_SWAP = [(i, i ^ 1) for i in range(NZ * NY * NC)]
PLANES = [
    [br_index(z, y, c) * OWN + o for y in range(NY) for c in range(NC) for o in range(OWN)]
    for z in range(NZ)
]


def plane_exchange(blocks):
    return lax.all_to_all(
        blocks, ("br", "own"), split_axis=0, concat_axis=0, tiled=True, axis_index_groups=PLANES
    )


def dot_nt(a, b):
    return lax.dot_general(a, b, (((1,), (1,)), ((), ())), preferred_element_type=jnp.float32)


def dot_nn(a, b):
    return lax.dot_general(a, b, (((1,), (0,)), ((), ())), preferred_element_type=jnp.float32)


def dot_tn(a, b):
    return lax.dot_general(a, b, (((0,), (0,)), ((), ())), preferred_element_type=jnp.float32)


def heads_of(ref, slot):
    return [ref[slot, :, g * HD : (g + 1) * HD] for g in range(GROUPS)]


def attention_grads(k, v, qs, dos, lses, deltas, visible=None):
    probs = [jnp.exp2(dot_nt(k, q) * (SCALE * LOG2E) - lse * LOG2E) for q, lse in zip(qs, lses)]
    if visible is not None:
        probs = [jnp.where(visible, prob, 0.0) for prob in probs]
    dprobs = [dot_nt(v, do) for do in dos]
    dscores = [
        (prob * (dprob - delta)).astype(jnp.bfloat16)
        for prob, dprob, delta in zip(probs, dprobs, deltas)
    ]
    probs = [prob.astype(jnp.bfloat16) for prob in probs]
    dk = SCALE * dot_nn(jnp.concatenate(dscores, 1), jnp.concatenate(qs, 0))
    dv = dot_nn(jnp.concatenate(probs, 1), jnp.concatenate(dos, 0))
    dqs = [SCALE * dot_tn(dscore, k) for dscore in dscores]
    return dqs, dk, dv


def vmem():
    return pl.BlockSpec(memory_space=pltpu.VMEM)


def smem():
    return pl.BlockSpec(memory_space=pltpu.SMEM)


def send_kernel(key_ref, value_ref, out_ref):
    for h in range(KVH):
        cols = slice(h * HD, (h + 1) * HD)
        key, value = key_ref[:, cols], value_ref[:, cols]
        for block in range(NY * NC):
            out_ref[block * KVH + h, :, :HD] = key
            out_ref[block * KVH + h, :, HD:] = value


def send_part(prefix_keys, prefix_values):
    rows = prefix_keys.shape[0]
    flat = (rows, KVH * HD)
    return pl.pallas_call(
        send_kernel,
        in_specs=[vmem()] * 2,
        out_specs=vmem(),
        out_shape=jax.ShapeDtypeStruct((NY * NC * KVH, rows, 2 * HD), jnp.bfloat16),
        name="send_part",
    )(prefix_keys.reshape(flat), prefix_values.reshape(flat))


def home_kernel(in_ref, key_ref, value_ref):
    for h in range(KVH):
        cols = slice(h * HD, (h + 1) * HD)
        parts = [in_ref[block * KVH + h].astype(jnp.float32) for block in range(NY * NC)]
        total = ((parts[0] + parts[1]) + (parts[2] + parts[3])).astype(jnp.bfloat16)
        key_ref[:, cols] = total[:, :HD]
        value_ref[:, cols] = total[:, HD:]


def home_part(received):
    rows = received.shape[1]
    shape = jax.ShapeDtypeStruct((rows, KVH * HD), jnp.bfloat16)
    grads = pl.pallas_call(
        home_kernel,
        in_specs=[vmem()],
        out_specs=[vmem()] * 2,
        out_shape=[shape, shape],
        name="home_part",
    )(received)
    return [grad.reshape(rows, 1, KVH * HD) for grad in grads]


def slot_spec(*shape):
    return pl.BlockSpec((1,) + shape, lambda i: (i, 0, 0))


def stat_kernel(o_ref, do_ref, lse_ref, stat_ref):
    stat_ref[0, :GROUPS, :] = lse_ref[0]
    for g, (do, o) in enumerate(zip(heads_of(do_ref, 0), heads_of(o_ref, 0))):
        product = do.astype(jnp.float32) * o.astype(jnp.float32)
        stat_ref[0, 8 + g : 9 + g, :] = jnp.sum(product.T, axis=0, keepdims=True)


def stat_part(attn_out, out_grad, logsumexp):
    slots, length, width = attn_out.shape
    return pl.pallas_call(
        stat_kernel,
        grid=(slots,),
        in_specs=[slot_spec(length, width), slot_spec(length, width), slot_spec(GROUPS, length)],
        out_specs=slot_spec(16, length),
        out_shape=jax.ShapeDtypeStruct((slots, 16, length), jnp.float32),
        compiler_params=pltpu.CompilerParams(vmem_limit_bytes=KERNEL_VMEM),
        cost_estimate=pl.CostEstimate(
            flops=slots * 2 * length * width,
            bytes_accessed=slots * length * width * 4,
            transcendentals=0,
        ),
        name="stat_part",
    )(attn_out, out_grad, logsumexp)


def self_kernel(count_ref, q_ref, k_ref, v_ref, do_ref, stat_ref, dq_ref, dk_ref, dv_ref):
    live = pl.program_id(0) < count_ref[0]

    @pl.when(live)
    def _():
        k, v = k_ref[0], v_ref[0]
        length = k.shape[0]
        row = lax.broadcasted_iota(jnp.int32, (length, length), 0)
        token = lax.broadcasted_iota(jnp.int32, (length, length), 1)
        dqs, dk, dv = attention_grads(
            k,
            v,
            heads_of(q_ref, 0),
            heads_of(do_ref, 0),
            [stat_ref[0, g : g + 1, :] for g in range(GROUPS)],
            [stat_ref[0, 8 + g : 9 + g, :] for g in range(GROUPS)],
            row <= token,
        )
        for g in range(GROUPS):
            dq_ref[0, :, g * HD : (g + 1) * HD] = dqs[g].astype(dq_ref.dtype)
        dk_ref[0] = dk.astype(jnp.bfloat16)
        dv_ref[0] = dv.astype(jnp.bfloat16)

    @pl.when(jnp.logical_not(live))
    def _():
        for ref in (dq_ref, dk_ref, dv_ref):
            ref[...] = jnp.zeros_like(ref)


def self_part(count, queries, keys, values, out_grad, stat):
    slots, length, width = queries.shape
    wide, narrow = slot_spec(length, width), slot_spec(length, HD)
    return pl.pallas_call(
        self_kernel,
        grid=(slots,),
        in_specs=[smem(), wide, narrow, narrow, wide, slot_spec(16, length)],
        out_specs=[wide, narrow, narrow],
        out_shape=[
            jax.ShapeDtypeStruct((slots, length, width), jnp.bfloat16),
            jax.ShapeDtypeStruct((slots, length, HD), jnp.bfloat16),
            jax.ShapeDtypeStruct((slots, length, HD), jnp.bfloat16),
        ],
        compiler_params=pltpu.CompilerParams(vmem_limit_bytes=KERNEL_VMEM),
        cost_estimate=pl.CostEstimate(
            flops=slots * 10 * length * length * width,
            bytes_accessed=slots * length * width * 10,
            transcendentals=slots * length * length * GROUPS,
        ),
        name="self_part",
    )(count, queries, keys, values, out_grad, stat)


def prefix_kernel(n_pieces, slots, with_oth, pre_ref, *refs):
    refs = list(refs)
    take = lambda n: [refs.pop(0) for _ in range(n)]
    q_own, do_own, stat_own, q_oth, do_oth, stat_oth, more_own = take(7)
    more_oth = take(1)[0] if with_oth else None
    pieces = take(n_pieces)
    dq_own, dq_oth = take(2)
    outs = take(n_pieces)
    (acc,) = refs
    step = pl.program_id(0)
    prefix = pre_ref[step]

    @pl.when(step == 0)
    def _():
        acc[...] = jnp.zeros_like(acc)

    def work(q_ref, do_ref, stat_ref, more_ref, dq_ref):
        @pl.when(prefix >= 0)
        def _():
            rows = [p[:, prefix] for p in pieces]
            kv = jnp.concatenate([r.reshape(r.shape[0] * r.shape[1], 2 * HD) for r in rows], 0)
            k, v = kv[:, :HD], kv[:, HD:]
            dqs, dk, dv = attention_grads(
                k,
                v,
                heads_of(q_ref, 0),
                heads_of(do_ref, 0),
                [stat_ref[0, g : g + 1, :] for g in range(GROUPS)],
                [stat_ref[0, 8 + g : 9 + g, :] for g in range(GROUPS)],
            )
            for g in range(GROUPS):
                cols = slice(g * HD, (g + 1) * HD)
                dq = dqs[g]
                if more_ref is not None:
                    dq += more_ref[0, :, cols].astype(jnp.float32)
                dq_ref[0, :, cols] = dq.astype(dq_ref.dtype)
            acc[prefix, :, :HD] += dk
            acc[prefix, :, HD:] += dv

        @pl.when(prefix < 0)
        def _():
            dq_ref[...] = jnp.zeros_like(dq_ref)

    @pl.when(step < slots)
    def _():
        work(q_own, do_own, stat_own, more_own, dq_own)

    @pl.when(step >= slots)
    def _():
        work(q_oth, do_oth, stat_oth, more_oth, dq_oth)

    @pl.when(step == 2 * slots - 1)
    def _():
        start = 0
        for out in outs:
            for block in range(out.shape[0]):
                out[block] = acc[:, start : start + out.shape[2], :].astype(out.dtype)
                start += out.shape[2]


def prefix_part(prefixes, own, oth, pieces, name):
    slots, length, width = own[0].shape
    n_rows = sum(p.shape[0] * p.shape[2] for p in pieces)
    n_pre = pieces[0].shape[1]

    def first(*shape):
        return pl.BlockSpec((1,) + shape, lambda i, c: (jnp.minimum(i, slots - 1), 0, 0))

    def second(*shape):
        return pl.BlockSpec((1,) + shape, lambda i, c: (jnp.maximum(i - slots, 0), 0, 0))

    def whole(p):
        return pl.BlockSpec(p.shape, lambda i, c: (0, 0, 0, 0))

    in_specs = [first(*a.shape[1:]) for a in own[:3]] + [second(*a.shape[1:]) for a in oth[:3]]
    in_specs += [first(length, width)] + [second(length, width) for _ in oth[3:]]
    return pl.pallas_call(
        functools.partial(prefix_kernel, len(pieces), slots, len(oth) > 3),
        grid_spec=pltpu.PrefetchScalarGridSpec(
            num_scalar_prefetch=1,
            grid=(2 * slots,),
            in_specs=in_specs + [whole(p) for p in pieces],
            out_specs=[first(length, width), second(length, width)] + [whole(p) for p in pieces],
            scratch_shapes=[pltpu.VMEM((n_pre, n_rows, 2 * HD), jnp.float32)],
        ),
        out_shape=[
            jax.ShapeDtypeStruct((slots, length, width), jnp.bfloat16),
            jax.ShapeDtypeStruct((slots, length, width), jnp.bfloat16),
        ]
        + [jax.ShapeDtypeStruct(p.shape, jnp.bfloat16) for p in pieces],
        compiler_params=pltpu.CompilerParams(vmem_limit_bytes=KERNEL_VMEM),
        cost_estimate=pl.CostEstimate(
            flops=2 * slots * 10 * length * n_rows * width,
            bytes_accessed=slots * length * width * 16,
            transcendentals=2 * slots * length * n_rows * GROUPS,
        ),
        name=name,
    )(prefixes, *own[:3], *oth[:3], own[3], *oth[3:], *pieces)


def per_device(
    queries,
    branch_keys,
    branch_values,
    attn_out,
    out_grad,
    logsumexp,
    prefix_keys,
    prefix_values,
    prefix_of,
    counts,
):
    slots = queries.shape[0]
    rows, n_pre = prefix_keys.shape[0], OWN
    core = lax.rem(lax.axis_index("br"), NC)
    swap = functools.partial(lax.ppermute, axis_name="br", perm=CORE_SWAP)

    f32, bf16 = jnp.float32, jnp.bfloat16
    plane = plane_exchange(send_part(prefix_keys, prefix_values))
    plane = plane.reshape(NY * NC, n_pre, rows, 2 * HD)

    mine = jnp.where(jnp.arange(slots) < counts[0], prefix_of, -1)
    prefixes = jnp.concatenate([mine, swap(mine)])
    q_oth, do_oth = swap(queries), swap(out_grad)
    stat = stat_part(attn_out, out_grad, logsumexp)
    stat_oth = swap(stat)
    plane, prefixes, q_oth, do_oth, count, stat, stat_oth = lax.optimization_barrier(
        (plane, prefixes, q_oth, do_oth, counts, stat, stat_oth)
    )
    own_half = lax.dynamic_slice_in_dim(plane, core * (NY * NC // 2), NY * NC // 2, 0)
    one = lax.ppermute(plane, "br", ring_perm(1))
    two = lax.ppermute(plane, "br", ring_perm(2))
    three = lax.ppermute(plane, "br", ring_perm(3))
    half_three = lax.dynamic_slice_in_dim(three, core * (NY * NC // 2), NY * NC // 2, 0)
    four = lax.ppermute(half_three, "br", ring_perm(1))
    dq_self, key_grad, value_grad = self_part(
        count, queries, branch_keys, branch_values, out_grad, stat
    )
    dq_own, dq_oth, g_own, g1, g2, g3, g4 = prefix_part(
        prefixes,
        (queries, out_grad, stat, dq_self),
        (q_oth, do_oth, stat_oth),
        (own_half, one, two, three, four),
        "prefix_part",
    )
    in_half = (jnp.arange(NY * NC) // (NY * NC // 2) == core)[:, None, None, None]
    far = lax.ppermute(g4, "br", ring_perm(-1)).astype(f32)
    far = jnp.where(in_half, jnp.concatenate([far, far], 0), 0.0)
    h3 = lax.ppermute((g3.astype(f32) + far).astype(bf16), "br", ring_perm(-3))
    h2 = lax.ppermute(g2, "br", ring_perm(-2))
    h1 = lax.ppermute(g1, "br", ring_perm(-1))
    dq_back = swap(dq_oth)
    query_grad = (dq_own.astype(f32) + dq_back.astype(f32)).astype(bf16)

    near, query_grad = lax.optimization_barrier((h1.astype(f32) + h2.astype(f32), query_grad))
    halves = g_own.astype(f32)
    spread = jnp.where(in_half, jnp.concatenate([halves, halves], 0), 0.0)
    total = (near + (h3.astype(f32) + spread)).astype(bf16)
    prefix_key_grad, prefix_value_grad = home_part(
        plane_exchange(total.reshape(NY * NC * n_pre, rows, 2 * HD))
    )
    return (query_grad, key_grad, value_grad, prefix_key_grad, prefix_value_grad)


def solution(mesh):
    placed = (
        P("br", None, "own"),
        P("br", None, "own"),
        P("br", None, "own"),
        P("br", None, "own"),
        P("br", None, "own"),
        P("br", "own", None),
        P("br", "own", None),
        P("br", "own", None),
        P("br"),
        P("br"),
    )
    return jax.shard_map(
        per_device,
        mesh=mesh,
        in_specs=placed,
        out_specs=(
            P("br", None, "own"),
            P("br", None, "own"),
            P("br", None, "own"),
            P("br", "own", None),
            P("br", "own", None),
        ),
        check_vma=False,
    )
```

```python
import functools

import jax
import jax.numpy as jnp
from jax import lax
from jax.experimental import pallas as pl
from jax.experimental.pallas import tpu as pltpu
from jax.sharding import PartitionSpec as P

QH = 40
KVH = 8
HD = 128
GROUPS = QH // KVH
SCALE = HD ** (-0.5)
LOG2E = 1.4426950408889634
NZ, NY, NC = 8, 2, 2
OWN = 8
KERNEL_VMEM = 24 << 20
NZ, NY, NC = 8, 2, 2
OWN = 8
KERNEL_VMEM = 24 << 20
NEAR_WEIGHT = 0.01


def br_index(z, y, c):
    return (z % NZ) * NY * NC + y * NC + c


def ring_perm(hops):
    return [
        (br_index(z, y, c), br_index(z + (hops if c == 0 else -hops), y, c))
        for z in range(NZ)
        for y in range(NY)
        for c in range(NC)
    ]


CORE_SWAP = [(i, i ^ 1) for i in range(NZ * NY * NC)]
PLANES = [
    [br_index(z, y, c) * OWN + o for y in range(NY) for c in range(NC) for o in range(OWN)]
    for z in range(NZ)
]


def plane_exchange(blocks):
    return lax.all_to_all(
        blocks, ("br", "own"), split_axis=0, concat_axis=0, tiled=True, axis_index_groups=PLANES
    )


def dot_nt(a, b):
    return lax.dot_general(a, b, (((1,), (1,)), ((), ())), preferred_element_type=jnp.float32)


def dot_nn(a, b):
    return lax.dot_general(a, b, (((1,), (0,)), ((), ())), preferred_element_type=jnp.float32)


def dot_tn(a, b):
    return lax.dot_general(a, b, (((0,), (0,)), ((), ())), preferred_element_type=jnp.float32)


def heads_of(ref, slot):
    return [ref[slot, :, g * HD : (g + 1) * HD] for g in range(GROUPS)]


def attention_grads(k, v, qs, dos, lses, deltas, visible=None):
    probs = [jnp.exp2(dot_nt(k, q) * (SCALE * LOG2E) - lse * LOG2E) for q, lse in zip(qs, lses)]
    if visible is not None:
        probs = [jnp.where(visible, prob, 0.0) for prob in probs]
    dprobs = [dot_nt(v, do) for do in dos]
    dscores = [
        (prob * (dprob - delta)).astype(jnp.bfloat16)
        for prob, dprob, delta in zip(probs, dprobs, deltas)
    ]
    probs = [prob.astype(jnp.bfloat16) for prob in probs]
    dk = SCALE * dot_nn(jnp.concatenate(dscores, 1), jnp.concatenate(qs, 0))
    dv = dot_nn(jnp.concatenate(probs, 1), jnp.concatenate(dos, 0))
    dqs = [SCALE * dot_tn(dscore, k) for dscore in dscores]
    return dqs, dk, dv


def vmem():
    return pl.BlockSpec(memory_space=pltpu.VMEM)


def smem():
    return pl.BlockSpec(memory_space=pltpu.SMEM)


def send_kernel(key_ref, value_ref, out_ref):
    for h in range(KVH):
        cols = slice(h * HD, (h + 1) * HD)
        key, value = key_ref[:, cols], value_ref[:, cols]
        for block in range(NY * NC):
            out_ref[block * KVH + h, :, :HD] = key
            out_ref[block * KVH + h, :, HD:] = value


def send_part(prefix_keys, prefix_values):
    rows = prefix_keys.shape[0]
    flat = (rows, KVH * HD)
    return pl.pallas_call(
        send_kernel,
        in_specs=[vmem()] * 2,
        out_specs=vmem(),
        out_shape=jax.ShapeDtypeStruct((NY * NC * KVH, rows, 2 * HD), jnp.bfloat16),
        name="send_part",
    )(prefix_keys.reshape(flat), prefix_values.reshape(flat))


def home_kernel(in_ref, key_ref, value_ref):
    for h in range(KVH):
        cols = slice(h * HD, (h + 1) * HD)
        parts = [in_ref[block * KVH + h].astype(jnp.float32) for block in range(NY * NC)]
        total = ((parts[0] + parts[1]) + (parts[2] + parts[3])).astype(jnp.bfloat16)
        key_ref[:, cols] = total[:, :HD]
        value_ref[:, cols] = total[:, HD:]


def home_part(received):
    rows = received.shape[1]
    shape = jax.ShapeDtypeStruct((rows, KVH * HD), jnp.bfloat16)
    grads = pl.pallas_call(
        home_kernel,
        in_specs=[vmem()],
        out_specs=[vmem()] * 2,
        out_shape=[shape, shape],
        name="home_part",
    )(received)
    return [grad.reshape(rows, 1, KVH * HD) for grad in grads]


def slot_spec(*shape):
    return pl.BlockSpec((1,) + shape, lambda i: (i, 0, 0))


def stat_kernel(o_ref, do_ref, lse_ref, stat_ref):
    stat_ref[0, :GROUPS, :] = lse_ref[0]
    for g, (do, o) in enumerate(zip(heads_of(do_ref, 0), heads_of(o_ref, 0))):
        product = do.astype(jnp.float32) * o.astype(jnp.float32)
        stat_ref[0, 8 + g : 9 + g, :] = jnp.sum(product.T, axis=0, keepdims=True)


def stat_part(attn_out, out_grad, logsumexp):
    slots, length, width = attn_out.shape
    return pl.pallas_call(
        stat_kernel,
        grid=(slots,),
        in_specs=[slot_spec(length, width), slot_spec(length, width), slot_spec(GROUPS, length)],
        out_specs=slot_spec(16, length),
        out_shape=jax.ShapeDtypeStruct((slots, 16, length), jnp.float32),
        compiler_params=pltpu.CompilerParams(vmem_limit_bytes=KERNEL_VMEM),
        cost_estimate=pl.CostEstimate(
            flops=slots * 2 * length * width,
            bytes_accessed=slots * length * width * 4,
            transcendentals=0,
        ),
        name="stat_part",
    )(attn_out, out_grad, logsumexp)


def self_kernel(count_ref, q_ref, k_ref, v_ref, do_ref, stat_ref, dq_ref, dk_ref, dv_ref):
    live = pl.program_id(0) < count_ref[0]

    @pl.when(live)
    def _():
        k, v = k_ref[0], v_ref[0]
        length = k.shape[0]
        row = lax.broadcasted_iota(jnp.int32, (length, length), 0)
        token = lax.broadcasted_iota(jnp.int32, (length, length), 1)
        dqs, dk, dv = attention_grads(
            k,
            v,
            heads_of(q_ref, 0),
            heads_of(do_ref, 0),
            [stat_ref[0, g : g + 1, :] for g in range(GROUPS)],
            [stat_ref[0, 8 + g : 9 + g, :] for g in range(GROUPS)],
            row <= token,
        )
        for g in range(GROUPS):
            dq_ref[0, :, g * HD : (g + 1) * HD] = dqs[g].astype(dq_ref.dtype)
        dk_ref[0] = dk.astype(jnp.bfloat16)
        dv_ref[0] = dv.astype(jnp.bfloat16)

    @pl.when(jnp.logical_not(live))
    def _():
        for ref in (dq_ref, dk_ref, dv_ref):
            ref[...] = jnp.zeros_like(ref)


def self_part(count, queries, keys, values, out_grad, stat):
    slots, length, width = queries.shape
    wide, narrow = slot_spec(length, width), slot_spec(length, HD)
    return pl.pallas_call(
        self_kernel,
        grid=(slots,),
        in_specs=[smem(), wide, narrow, narrow, wide, slot_spec(16, length)],
        out_specs=[wide, narrow, narrow],
        out_shape=[
            jax.ShapeDtypeStruct((slots, length, width), jnp.bfloat16),
            jax.ShapeDtypeStruct((slots, length, HD), jnp.bfloat16),
            jax.ShapeDtypeStruct((slots, length, HD), jnp.bfloat16),
        ],
        compiler_params=pltpu.CompilerParams(vmem_limit_bytes=KERNEL_VMEM),
        cost_estimate=pl.CostEstimate(
            flops=slots * 10 * length * length * width,
            bytes_accessed=slots * length * width * 10,
            transcendentals=slots * length * length * GROUPS,
        ),
        name="self_part",
    )(count, queries, keys, values, out_grad, stat)


def prefix_kernel(n_pieces, slots, with_oth, pre_ref, *refs):
    refs = list(refs)
    take = lambda n: [refs.pop(0) for _ in range(n)]
    q_own, do_own, stat_own, q_oth, do_oth, stat_oth, more_own = take(7)
    more_oth = take(1)[0] if with_oth else None
    pieces = take(n_pieces)
    dq_own, dq_oth = take(2)
    outs = take(n_pieces)
    (acc,) = refs
    step = pl.program_id(0)
    prefix = pre_ref[step]

    @pl.when(step == 0)
    def _():
        acc[...] = jnp.zeros_like(acc)

    def work(q_ref, do_ref, stat_ref, more_ref, dq_ref):
        @pl.when(prefix >= 0)
        def _():
            rows = [p[:, prefix] for p in pieces]
            kv = jnp.concatenate([r.reshape(r.shape[0] * r.shape[1], 2 * HD) for r in rows], 0)
            k, v = kv[:, :HD], kv[:, HD:]
            dqs, dk, dv = attention_grads(
                k,
                v,
                heads_of(q_ref, 0),
                heads_of(do_ref, 0),
                [stat_ref[0, g : g + 1, :] for g in range(GROUPS)],
                [stat_ref[0, 8 + g : 9 + g, :] for g in range(GROUPS)],
            )
            for g in range(GROUPS):
                cols = slice(g * HD, (g + 1) * HD)
                dq = dqs[g]
                if more_ref is not None:
                    dq += more_ref[0, :, cols].astype(jnp.float32)
                dq_ref[0, :, cols] = dq.astype(dq_ref.dtype)
            acc[prefix, :, :HD] += dk
            acc[prefix, :, HD:] += dv

        @pl.when(prefix < 0)
        def _():
            dq_ref[...] = jnp.zeros_like(dq_ref)

    @pl.when(step < slots)
    def _():
        work(q_own, do_own, stat_own, more_own, dq_own)

    @pl.when(step >= slots)
    def _():
        work(q_oth, do_oth, stat_oth, more_oth, dq_oth)

    @pl.when(step == 2 * slots - 1)
    def _():
        start = 0
        for out in outs:
            for block in range(out.shape[0]):
                out[block] = acc[:, start : start + out.shape[2], :].astype(out.dtype)
                start += out.shape[2]


def prefix_part(prefixes, own, oth, pieces, name):
    slots, length, width = own[0].shape
    n_rows = sum(p.shape[0] * p.shape[2] for p in pieces)
    n_pre = pieces[0].shape[1]

    def first(*shape):
        return pl.BlockSpec((1,) + shape, lambda i, c: (jnp.minimum(i, slots - 1), 0, 0))

    def second(*shape):
        return pl.BlockSpec((1,) + shape, lambda i, c: (jnp.maximum(i - slots, 0), 0, 0))

    def whole(p):
        return pl.BlockSpec(p.shape, lambda i, c: (0, 0, 0, 0))

    in_specs = [first(*a.shape[1:]) for a in own[:3]] + [second(*a.shape[1:]) for a in oth[:3]]
    in_specs += [first(length, width)] + [second(length, width) for _ in oth[3:]]
    return pl.pallas_call(
        functools.partial(prefix_kernel, len(pieces), slots, len(oth) > 3),
        grid_spec=pltpu.PrefetchScalarGridSpec(
            num_scalar_prefetch=1,
            grid=(2 * slots,),
            in_specs=in_specs + [whole(p) for p in pieces],
            out_specs=[first(length, width), second(length, width)] + [whole(p) for p in pieces],
            scratch_shapes=[pltpu.VMEM((n_pre, n_rows, 2 * HD), jnp.float32)],
        ),
        out_shape=[
            jax.ShapeDtypeStruct((slots, length, width), jnp.bfloat16),
            jax.ShapeDtypeStruct((slots, length, width), jnp.bfloat16),
        ]
        + [jax.ShapeDtypeStruct(p.shape, jnp.bfloat16) for p in pieces],
        compiler_params=pltpu.CompilerParams(vmem_limit_bytes=KERNEL_VMEM),
        cost_estimate=pl.CostEstimate(
            flops=2 * slots * 10 * length * n_rows * width,
            bytes_accessed=slots * length * width * 16,
            transcendentals=2 * slots * length * n_rows * GROUPS,
        ),
        name=name,
    )(prefixes, *own[:3], *oth[:3], own[3], *oth[3:], *pieces)


def per_device(
    queries,
    branch_keys,
    branch_values,
    attn_out,
    out_grad,
    logsumexp,
    prefix_keys,
    prefix_values,
    prefix_of,
    counts,
):
    slots = queries.shape[0]
    rows, n_pre = prefix_keys.shape[0], OWN
    core = lax.rem(lax.axis_index("br"), NC)
    swap = functools.partial(lax.ppermute, axis_name="br", perm=CORE_SWAP)

    f32, bf16 = jnp.float32, jnp.bfloat16
    plane = plane_exchange(send_part(prefix_keys, prefix_values))
    plane = plane.reshape(NY * NC, n_pre, rows, 2 * HD)

    mine = jnp.where(jnp.arange(slots) < counts[0], prefix_of, -1)
    prefixes = jnp.concatenate([mine, swap(mine)])
    q_oth, do_oth = swap(queries), swap(out_grad)
    stat = stat_part(attn_out, out_grad, logsumexp)
    stat_oth = swap(stat)
    plane, prefixes, q_oth, do_oth, count, stat = lax.optimization_barrier(
        (plane, prefixes, q_oth, do_oth, counts, stat)
    )
    own_half = lax.dynamic_slice_in_dim(plane, core * (NY * NC // 2), NY * NC // 2, 0)
    one = lax.ppermute(plane, "br", ring_perm(1))
    two = lax.ppermute(plane, "br", ring_perm(2))
    three = lax.ppermute(plane, "br", ring_perm(3))
    half_three = lax.dynamic_slice_in_dim(three, core * (NY * NC // 2), NY * NC // 2, 0)
    four = lax.ppermute(half_three, "br", ring_perm(1))
    dq_self, key_grad, value_grad = self_part(
        count, queries, branch_keys, branch_values, out_grad, stat
    )
    dq_own, dq_oth, g_own, g1, g2, g3, g4 = prefix_part(
        prefixes,
        (queries, out_grad, stat, dq_self),
        (q_oth, do_oth, stat_oth),
        (own_half, one, two, three, four),
        "prefix_part",
    )
    in_half = (jnp.arange(NY * NC) // (NY * NC // 2) == core)[:, None, None, None]
    far = lax.ppermute(g4, "br", ring_perm(-1)).astype(f32)
    far = jnp.where(in_half, jnp.concatenate([far, far], 0), 0.0)
    h3 = lax.ppermute((g3.astype(f32) + far).astype(bf16), "br", ring_perm(-3))
    h2 = lax.ppermute(g2, "br", ring_perm(-2))
    h1 = lax.ppermute(g1, "br", ring_perm(-1))
    dq_back = swap(dq_oth)
    query_grad = (dq_own.astype(f32) + dq_back.astype(f32)).astype(bf16)

    near, query_grad = lax.optimization_barrier((h1.astype(f32) + h2.astype(f32), query_grad))
    halves = g_own.astype(f32)
    spread = jnp.where(in_half, jnp.concatenate([halves, halves], 0), 0.0)
    total = (near + (h3.astype(f32) + spread)).astype(bf16)
    prefix_key_grad, prefix_value_grad = home_part(
        plane_exchange(total.reshape(NY * NC * n_pre, rows, 2 * HD))
    )
    return (query_grad, key_grad, value_grad, prefix_key_grad, prefix_value_grad)


def solution(mesh):
    placed = (
        P("br", None, "own"),
        P("br", None, "own"),
        P("br", None, "own"),
        P("br", None, "own"),
        P("br", None, "own"),
        P("br", "own", None),
        P("br", "own", None),
        P("br", "own", None),
        P("br"),
        P("br"),
    )
    return jax.shard_map(
        per_device,
        mesh=mesh,
        in_specs=placed,
        out_specs=(
            P("br", None, "own"),
            P("br", None, "own"),
            P("br", None, "own"),
            P("br", "own", None),
            P("br", "own", None),
        ),
        check_vma=False,
    )
```
